128 devices in a mesh: row: 8 (over z, core), col: 16 (over x, y).
Axes of the slice: x: 4, y: 4, z: 4, core: 2. Of those that a mesh axis runs over, the one named last changes fastest.
Arguments:
- x_values: bfloat16 [1024, 12288], P('row', 'col'), may hold values from -6 to 6
- x_scales: bfloat16 [96, 1024], P('col', 'row'), may hold values from 0.25 to 4
- up_weight: bfloat16 [12288, 24576], P('col', 'row'), may hold values from -0.0546875 to 0.0546875
- down_weight: bfloat16 [24576, 12288], P('row', 'col'), may hold values from -0.0390625 to 0.0390625
- grad_values: bfloat16 [1024, 12288], P('row', 'col'), may hold values from -0.1875 to 0.1875
- grad_scales: bfloat16 [96, 1024], P('col', 'row'), may hold values from 0.25 to 4
Outputs:
- output: bfloat16 [1024, 12288], P('row', 'col')
- up_grad: float32 [12288, 24576], P('col', 'row')
The draws below stay inside these ranges and needn't reach their ends.
All inputs are finite; a program needn't handle non-finite values.
Results may differ from the reference program's by a relative error of at most 0.039.
Values may be sent and summed in bfloat16 or wider, within the bound.
No kernel may reach another device: no remote copies, remote signals or barrier semaphores. Data moves between devices by JAX's collectives and lax.ppermute only.
A program may use at most 128 MiB of HBM per device.

```python
import math
import jax
import jax.numpy as jnp
from jax import lax

D = 12288
FF = 24576
BLOCK = 128
TOKENS = 1024
N_COL = 16


def block_levels(rng, shape, pieces, least, high):
    def one(dim, shards_of):
        steps = jax.random.uniform(jax.random.fold_in(jax.random.fold_in(rng, 6), dim), (shards_of,), jnp.float32, least / len(pieces), high / len(pieces))
        return jnp.repeat(jnp.exp(steps), shape[dim] // shards_of).reshape((-1,) + (1,) * (len(shape) - dim - 1))

    factor_of = one(*pieces[0])
    for cut in pieces[1:]:
        factor_of = factor_of * one(*cut)
    return factor_of


def noise(own_key, shape, deviation, bound, pieces=(), kind=jnp.bfloat16):
    drawn = jax.random.normal(own_key, shape, jnp.float32) * deviation
    if len(pieces) > 0:
        drawn = block_levels(own_key, shape, pieces, -0.22, 0.18) * drawn
    return jnp.clip(drawn, min=-bound, max=bound).astype(kind)


def setup_inputs(seed: int = 0) -> dict:
    arg_keys = jax.random.split(jax.random.key(seed), 7)
    return {
        "x_values": noise(arg_keys[0], (TOKENS, D), 1.0, 6.0, ((0, 8), (1, 16))),
        "x_scales": jnp.clip(jnp.exp(math.log(4.0) - 2.7725887 * jax.random.uniform(arg_keys[1], (D // BLOCK, TOKENS), jnp.float32) ** block_levels(arg_keys[1], (D // BLOCK, TOKENS), ((0, 16), (1, 8)), -0.2, 0.2)), 0.25, 4.0).astype(jnp.bfloat16),
        "up_weight": noise(arg_keys[2], (D, FF), D ** -0.5, 0.0546875, ((0, 16), (1, 8))),
        "down_weight": noise(arg_keys[3], (FF, D), FF ** -0.5, 0.0390625, ((0, 8), (1, 16))),
        "grad_values": noise(arg_keys[4], (TOKENS, D), (TOKENS ** -0.5), 0.1875, ((0, 8), (1, 16))),
        "grad_scales": jnp.clip(jnp.exp(math.log(4.0) - 2.7725887 * jax.random.uniform(arg_keys[5], (D // BLOCK, TOKENS), jnp.float32) ** block_levels(arg_keys[5], (D // BLOCK, TOKENS), ((0, 16), (1, 8)), -0.2, 0.2)), 0.25, 4.0).astype(jnp.bfloat16),
    }


def gelu(v):
    return 0.5 * v * (1.0 + jnp.tanh(0.7978845608 * (v + 0.044715 * v * v * v)))

def gelu_slope(v):
    return jax.vjp(gelu, v)[1](jnp.ones_like(v))[0]

def dequant(values, scales):
    count, width = values.shape
    blocks = values.astype(jnp.float32).reshape(count, width // BLOCK, BLOCK)
    scaled = blocks * scales.astype(jnp.float32).T[:, :, None]
    return scaled.reshape(count, width).astype(jnp.bfloat16)

def group_sum(left, right, contract_right):
    group = D // N_COL
    left_groups = left.reshape(left.shape[0], N_COL, group).transpose(1, 0, 2)

    def add_group(total, index):
        piece = lax.dynamic_slice_in_dim(left_groups, index, 1, 0)[0]
        if contract_right == 0:
            other = lax.dynamic_slice_in_dim(right, index * group, group, 0)
            term = jnp.dot(piece, other, preferred_element_type=jnp.float32)
        else:
            other = lax.dynamic_slice_in_dim(right, index * group, group, 1)
            term = lax.dot_general(piece, other, (((1,), (1,)), ((), ())), preferred_element_type=jnp.float32)
        return (total + term.astype(jnp.bfloat16).astype(jnp.float32), None)
    start = jnp.zeros((left.shape[0], FF), jnp.float32)
    total, unused = lax.scan(add_group, start, jnp.arange(N_COL, dtype=jnp.int32))
    return total

def reference(x_values, x_scales, up_weight, down_weight, grad_values, grad_scales):
    inputs = dequant(x_values, x_scales)
    cotangent = dequant(grad_values, grad_scales)
    pre = group_sum(inputs, up_weight, 0)
    hidden = gelu(pre).astype(jnp.bfloat16)
    output = jnp.dot(hidden, down_weight, preferred_element_type=jnp.float32).astype(jnp.bfloat16)
    grad_hidden = group_sum(cotangent, down_weight, 1)
    grad_pre = (grad_hidden * gelu_slope(pre)).astype(jnp.bfloat16)
    up_grad = lax.dot_general(inputs, grad_pre, (((0,), (0,)), ((), ())), preferred_element_type=jnp.float32)
    return (output, up_grad)
```

```python
import jax
import jax.numpy as jnp
from jax import lax
from jax.sharding import PartitionSpec as P

BLOCK = 128
SIDE = 4
BF16 = jnp.bfloat16
F32 = jnp.float32


def gelu(v):
    return 0.5 * v * (1.0 + jnp.tanh(0.7978845608 * (v + 0.044715 * v * v * v)))


def gelu_slope(v):
    return jax.vjp(gelu, v)[1](jnp.ones_like(v))[0]


def dequant(values, scales):
    count, width = values.shape
    blocks = values.astype(F32).reshape(count, width // BLOCK, BLOCK)
    scaled = blocks * scales.astype(F32).T[:, :, None]
    return scaled.reshape(count, width).astype(BF16)


def shift_perm(axis, step):
    if axis == "x":
        return [(4 * x + y, 4 * ((x + step) % 4) + y) for x in range(4) for y in range(4)]
    return [(4 * x + y, 4 * x + (y + step) % 4) for x in range(4) for y in range(4)]


def shift(a, axis, step):
    return lax.ppermute(a, "col", shift_perm(axis, step))


def z_shift(a, step):
    perm = [(2 * z + c, 2 * ((z + step) % 4) + c) for z in range(4) for c in range(2)]
    return lax.ppermute(a, "row", perm)


def core_swap(a):
    return lax.ppermute(a, "row", [(r, r ^ 1) for r in range(8)])


def rows(a, slot, size):
    return lax.dynamic_slice_in_dim(a, lax.rem(slot, SIDE) * size, size, 0)


def ring_sum(part, place, axis, way):
    far = shift(part(place + 2).astype(BF16), axis, way)
    back = shift(part(place + SIDE - way).astype(BF16), axis, -way)
    on = shift((part(place + SIDE + way) + far.astype(F32)).astype(BF16), axis, way)
    return part(place) + back.astype(F32) + on.astype(F32)


def ring_gather(mine, place, axis, way):
    before = shift(mine, axis, way)
    after = shift(mine, axis, -way)
    far = shift(before, axis, way)
    return [
        (place, mine),
        (place + SIDE - way, before),
        (place + SIDE + way, after),
        (place + 2, far),
    ]


def assemble(blocks):
    size = blocks[0][1].shape[0]
    out = jnp.zeros((SIDE * size,) + blocks[0][1].shape[1:], blocks[0][1].dtype)
    for slot, block in blocks:
        out = lax.dynamic_update_slice_in_dim(out, block, lax.rem(slot, SIDE) * size, 0)
    return out


def gather_rows(own):
    up = z_shift(own, -1)
    down = z_shift(own, 1)
    far = z_shift(own, 2)
    same = jnp.concatenate([own, up, far, down], axis=0)
    return jnp.concatenate([same, core_swap(same)], axis=0)


def local(x_values, x_scales, up_weight, down_weight, grad_values, grad_scales):
    col = lax.axis_index("col")
    at = {"x": col // SIDE, "y": lax.rem(col, SIDE)}
    inputs = gather_rows(dequant(x_values, x_scales))
    cotangent = gather_rows(dequant(grad_values, grad_scales))
    tokens, width = inputs.shape
    units = up_weight.shape[1]
    quarter = units // 4
    streams = [("x", "y", 1), ("x", "y", -1), ("y", "x", 1), ("y", "x", -1)]
    big, small = tokens // SIDE, tokens // SIDE // SIDE

    def scatter_sum(dot, stream):
        first, second, way = stream
        total = ring_sum(dot, at[first], first, way)
        return ring_sum(lambda slot: rows(total, slot, small), at[second], second, way)

    def gather(block, stream):
        first, second, way = stream
        return ring_gather(
            assemble(ring_gather(block, at[second], second, way)), at[first], first, way
        )

    pres, hiddens, grads = [], [], []
    for q, stream in enumerate(streams):
        weight = up_weight[:, q * quarter : (q + 1) * quarter]
        pre = scatter_sum(
            lambda slot: jnp.dot(rows(inputs, slot, big), weight, preferred_element_type=F32), stream
        )
        pres.append(pre)
        hiddens.append(gelu(pre).astype(BF16))
    for q, stream in enumerate(streams):
        weight = down_weight[q * quarter : (q + 1) * quarter]
        grads.append(
            scatter_sum(
                lambda slot: lax.dot_general(
                    rows(cotangent, slot, big),
                    weight,
                    (((1,), (1,)), ((), ())),
                    preferred_element_type=F32,
                ),
                stream,
            )
        )

    def spread(parts):
        whole = jnp.zeros((tokens, units), BF16)
        for q, stream in enumerate(streams):
            for slot, block in gather(parts[q], stream):
                whole = lax.dynamic_update_slice(
                    whole, block, (lax.rem(slot, SIDE) * big, q * quarter)
                )
        return whole

    terms = jnp.dot(spread(hiddens), down_weight, preferred_element_type=F32)
    half = tokens // 2
    mine = terms[:half] + core_swap(terms[half:].astype(BF16)).astype(F32)
    n = half // 4
    far = z_shift(mine[2 * n : 3 * n].astype(BF16), 2)
    up = z_shift(mine[n : 2 * n].astype(BF16), 1)
    down = z_shift(mine[3 * n :].astype(BF16), -1)
    output = (
        mine[:n] + far.astype(F32) + up.astype(F32) + down.astype(F32)
    ).astype(BF16)

    grad_pres = [
        (g * gelu_slope(p)).astype(BF16) for g, p in zip(grads, pres)
    ]
    up_grad = lax.dot_general(
        inputs, spread(grad_pres), (((0,), (0,)), ((), ())), preferred_element_type=F32
    )
    return (output, up_grad)


def solution(mesh):
    placed = (
        P("row", "col"),
        P("col", "row"),
        P("col", "row"),
        P("row", "col"),
        P("row", "col"),
        P("col", "row"),
    )
    return jax.shard_map(
        local,
        mesh=mesh,
        in_specs=placed,
        out_specs=(P("row", "col"), P("col", "row")),
        check_vma=False,
    )
```

```python
import jax
import jax.numpy as jnp
from jax import lax
from jax.sharding import PartitionSpec as P

BLOCK = 128
SIDE = 4
BF16 = jnp.bfloat16
F32 = jnp.float32


def gelu(v):
    return 0.5 * v * (1.0 + jnp.tanh(0.7978845608 * (v + 0.044715 * v * v * v)))


def gelu_slope(v):
    return jax.vjp(gelu, v)[1](jnp.ones_like(v))[0]


def dequant(values, scales):
    count, width = values.shape
    blocks = values.astype(F32).reshape(count, width // BLOCK, BLOCK)
    scaled = blocks * scales.astype(F32).T[:, :, None]
    return scaled.reshape(count, width).astype(BF16)


def steps_on(axis, step):
    if axis == "x":
        return [(4 * x + y, 4 * ((x + step) % 4) + y) for x in range(4) for y in range(4)]
    if axis == "y":
        return [(4 * x + y, 4 * x + (y + step) % 4) for x in range(4) for y in range(4)]
    if axis == "z":
        return [(2 * z + c, 2 * ((z + step) % 4) + c) for z in range(4) for c in range(2)]
    return [(r, r ^ 1) for r in range(8)]


def send(a, axis, step):
    return lax.ppermute(a, "col" if axis in ("x", "y") else "row", steps_on(axis, step))


def trade(*sends):
    held = lax.optimization_barrier([a for a, _, _ in sends])
    return [send(a, axis, step) for a, (_, axis, step) in zip(held, sends)]


def rows(a, slot, size):
    return lax.dynamic_slice_in_dim(a, lax.rem(slot, SIDE) * size, size, 0)


def far_halves(part, place):
    return [part(place + 2, h).astype(BF16) for h in range(2)]


def finish_sum(part, place, axis, got):
    low, high = got
    cut = low.shape[1]
    after, before, mine = lax.optimization_barrier(
        [part(place + 1, None).astype(BF16), part(place + 3, None).astype(BF16), part(place, None)]
    )
    after = after.at[:, :cut].add(low)
    before = before.at[:, cut:].add(high)
    return [mine] + trade((after, axis, 1), (before, axis, -1))


def narrow_sum(terms, place, axis):
    size = terms[0].shape[0] // SIDE

    def block(slot):
        return sum(rows(term, slot, size).astype(F32) for term in terms)

    got = trade(
        (block(place + 2).astype(BF16), axis, 2),
        (block(place + 1).astype(BF16), axis, 1),
        (block(place + 3).astype(BF16), axis, -1),
    )
    return block(place) + got[0].astype(F32) + got[1].astype(F32) + got[2].astype(F32)


def put(blocks, size):
    out = jnp.zeros((SIDE * size,) + blocks[0][1].shape[1:], blocks[0][1].dtype)
    for slot, block in blocks:
        out = lax.dynamic_update_slice_in_dim(out, block, lax.rem(slot, SIDE) * size, 0)
    return out


def narrow_gather(mine, place, axis):
    far, before, after = trade((mine, axis, 2), (mine, axis, 1), (mine, axis, -1))
    blocks = [(place, mine), (place + 2, far), (place + 3, before), (place + 1, after)]
    return put(blocks, mine.shape[0])


def wide_gather(mine, place, axis):
    n = mine.shape[0] // 2
    before, after = trade((mine, axis, 1), (mine, axis, -1))
    far = trade((before[:n], axis, 1), (after[n:], axis, -1))
    return [
        (place, 0, mine),
        (place + 3, 0, before),
        (place + 1, 0, after),
        (place + 2, 0, far[0]),
        (place + 2, n, far[1]),
    ]


def crosswise(a):
    split = a.reshape(SIDE, SIDE, a.shape[0] // SIDE // SIDE, a.shape[1])
    return split.transpose(1, 0, 2, 3).reshape(a.shape)


def z_sends(own):
    return [(own, "z", 2), (own, "z", -1), (own, "z", 1)]


def all_rows(own, got):
    same = jnp.concatenate([own, got[1], got[0], got[2]], axis=0)
    return jnp.concatenate([same, send(same, "core", 1)], axis=0)


def local(x_values, x_scales, up_weight, down_weight, grad_values, grad_scales):
    col = lax.axis_index("col")
    x, y = col // SIDE, lax.rem(col, SIDE)
    x_own = dequant(x_values, x_scales)
    x_z = trade(*z_sends(x_own))
    g_own, x_z[1] = lax.optimization_barrier((dequant(grad_values, grad_scales), x_z[1]))
    g_z = trade(*z_sends(g_own))
    inputs = all_rows(x_own, x_z)
    own = x_values.shape[0]
    tokens = inputs.shape[0]
    big = tokens // SIDE
    cut = up_weight.shape[1] // 2

    def up_part(slot, h):
        weight = up_weight if h is None else up_weight[:, h * cut : (h + 1) * cut]
        return jnp.dot(rows(inputs, slot, big), weight, preferred_element_type=F32)

    def down_part(slot, h):
        weight = down_weight if h is None else down_weight[h * cut : (h + 1) * cut]
        return lax.dot_general(
            rows(cotangent, slot, big), weight, (((1,), (1,)), ((), ())), preferred_element_type=F32
        )

    x_far = far_halves(up_part, x)
    x_got = trade((x_far[0], "x", 1), (x_far[1], "x", -1))
    cotangent = crosswise(all_rows(g_own, g_z))
    g_far = far_halves(down_part, y)
    g_got = trade((g_far[0], "y", 1), (g_far[1], "y", -1))
    pre = narrow_sum(finish_sum(up_part, x, "x", x_got), y, "y")
    hidden = wide_gather(narrow_gather(gelu(pre).astype(BF16), y, "y"), x, "x")
    grad = narrow_sum(finish_sum(down_part, y, "y", g_got), x, "x")
    grad_pre = (grad * gelu_slope(pre)).astype(BF16)
    grad_pre = wide_gather(narrow_gather(grad_pre, x, "x"), y, "y")

    terms = jnp.zeros((tokens, down_weight.shape[1]), F32)
    for slot, ahead, block in hidden:
        term = jnp.dot(block, down_weight, preferred_element_type=F32)
        terms = lax.dynamic_update_slice_in_dim(terms, term, lax.rem(slot, SIDE) * big + ahead, 0)
    middle, n = tokens // 2, own
    mine = terms[:middle] + send(terms[middle:].astype(BF16), "core", 1).astype(F32)
    sends = mine.astype(BF16)
    got = trade(
        (sends[2 * n : 3 * n], "z", 2), (sends[n : 2 * n], "z", 1), (sends[3 * n :], "z", -1)
    )
    output = mine[:n] + got[0].astype(F32) + got[1].astype(F32) + got[2].astype(F32)
    crossed = crosswise(inputs)
    whole = jnp.zeros((tokens, 2 * cut), BF16)
    for slot, ahead, block in grad_pre:
        whole = lax.dynamic_update_slice_in_dim(whole, block, lax.rem(slot, SIDE) * big + ahead, 0)
    up_grad = lax.dot_general(
        crossed, whole, (((0,), (0,)), ((), ())), preferred_element_type=F32
    )
    return (output.astype(BF16), up_grad)


def solution(mesh):
    placed = (
        P("row", "col"),
        P("col", "row"),
        P("col", "row"),
        P("row", "col"),
        P("row", "col"),
        P("col", "row"),
    )
    return jax.shard_map(
        local,
        mesh=mesh,
        in_specs=placed,
        out_specs=(P("row", "col"), P("col", "row")),
        check_vma=False,
    )
```

```python
import functools

import jax
import jax.numpy as jnp
from jax import lax
from jax.experimental import pallas as pl
from jax.experimental.pallas import tpu as pltpu
from jax.sharding import PartitionSpec as P

BLOCK = 128
SIDE = 4
TILES = 6
BF16 = jnp.bfloat16
F32 = jnp.float32
COST = pl.CostEstimate(flops=1000, bytes_accessed=1000, transcendentals=0)


def gelu(v):
    return 0.5 * v * (1.0 + jnp.tanh(0.7978845608 * (v + 0.044715 * v * v * v)))


def gelu_slope(v):
    return jax.vjp(gelu, v)[1](jnp.ones_like(v))[0]


def scale_kernel(xv_ref, xs_ref, gv_ref, gs_ref, out_ref):
    n = xv_ref.shape[0]
    i = lax.broadcasted_iota(jnp.int32, (n, n), 0)
    diagonal = i == lax.broadcasted_iota(jnp.int32, (n, n), 1)
    for t, (values, scales) in enumerate(((xv_ref, xs_ref), (gv_ref, gs_ref))):
        for b in range(values.shape[1] // BLOCK):
            at = slice(b * BLOCK, (b + 1) * BLOCK)
            row = scales[b : b + 1, :].astype(F32)
            weight = jnp.where(diagonal, jnp.broadcast_to(row, (n, n)), 0.0).astype(BF16)
            block = jnp.dot(weight, values[:, at], preferred_element_type=F32)
            out_ref[t * n : (t + 1) * n, at] = block.astype(BF16)


def scaled(x_values, x_scales, grad_values, grad_scales):
    n, width = x_values.shape
    return pl.pallas_call(
        scale_kernel, out_shape=jax.ShapeDtypeStruct((2 * n, width), BF16), name="scale"
    )(x_values, x_scales, grad_values, grad_scales)


def share_dot(tensor, take, same_ref, other_ref, w_ref):
    width = same_ref.shape[-1]
    if tensor == 0:
        a = jnp.concatenate([r[...].reshape(-1, width) for r in (same_ref, other_ref)], axis=0)
    else:
        a = jnp.where(take == 0, same_ref[...], other_ref[...]).reshape(-1, width)
    dims = (((1,), (tensor,)), ((), ()))
    return lax.dot_general(a, w_ref[...], dims, preferred_element_type=F32)


def core_of(slot_ref, step):
    return lax.div(lax.rem(slot_ref[0] + step, SIDE), 2)


def far_kernel(tensor, slot_ref, same_ref, other_ref, w_ref, low_ref, high_ref):
    j, half = pl.program_id(0), pl.num_programs(0) // 2
    out = share_dot(tensor, core_of(slot_ref, 2), same_ref, other_ref, w_ref).astype(BF16)

    @pl.when(j < half)
    def _():
        low_ref[...] = out

    @pl.when(j >= half)
    def _():
        high_ref[...] = out


def near_kernel(tensor, slot_ref, *refs):
    w_ref, outs = refs[6], refs[7:]
    for i, step in enumerate((1, 3, 0)):
        same_ref, other_ref = refs[2 * i : 2 * i + 2]
        out = share_dot(tensor, core_of(slot_ref, step), same_ref, other_ref, w_ref)
        outs[i][...] = out.astype(BF16)


def add_kernel(slot_ref, after_ref, before_ref, low_ref, high_ref, after_out, before_out):
    after_out[...] = (after_ref[...].astype(F32) + low_ref[...].astype(F32)).astype(BF16)
    before_out[...] = (before_ref[...].astype(F32) + high_ref[...].astype(F32)).astype(BF16)


def blocks_kernel(slots_ref, a_ref, b_ref, c_ref, *outs):
    total = sum(r[...].astype(F32) for r in (a_ref, b_ref, c_ref))
    for i, out in enumerate(outs):

        @pl.when(pl.program_id(0) == i)
        def _():
            out[...] = total.astype(out.dtype)


def row_blocks(terms, place):
    big, units = terms[0].shape
    small = big // SIDE
    slots = lax.rem(place + jnp.array([2, 1, 3, 0], jnp.int32), SIDE)
    grid = pltpu.PrefetchScalarGridSpec(
        num_scalar_prefetch=1,
        grid=(SIDE,),
        in_specs=[pl.BlockSpec((small, units), lambda j, slots: (slots[j], 0))] * 3,
        out_specs=[pl.BlockSpec((small, units), lambda j, slots: (0, 0))] * 4,
    )
    return pl.pallas_call(
        blocks_kernel,
        grid_spec=grid,
        out_shape=[pltpu.HBM((small, units), kind) for kind in (BF16, BF16, BF16, F32)],
        cost_estimate=COST,
        name="row_blocks",
    )(slots, *terms)


def act_kernel(a_ref, b_ref, c_ref, d_ref, pre_ref, hidden_ref):
    pre = a_ref[...] + sum(r[...].astype(F32) for r in (b_ref, c_ref, d_ref))
    pre_ref[...] = pre
    hidden_ref[...] = gelu(pre).astype(BF16)


def slope_kernel(a_ref, b_ref, c_ref, d_ref, pre_ref, out_ref):
    grad = a_ref[...] + sum(r[...].astype(F32) for r in (b_ref, c_ref, d_ref))
    out_ref[...] = (grad * gelu_slope(pre_ref[...])).astype(BF16)


def by_tiles(kernel, ins, kinds, name):
    rows_in, units = ins[0].shape
    spec = pl.BlockSpec((rows_in, units // 3), lambda j: (0, j))
    return pl.pallas_call(
        kernel,
        grid=(3,),
        in_specs=[spec] * len(ins),
        out_specs=[spec] * len(kinds),
        out_shape=[jax.ShapeDtypeStruct((rows_in, units), kind) for kind in kinds],
        cost_estimate=COST,
        name=name,
    )(*ins)


def put_kernel(slot_ref, mine_ref, far_ref, before_ref, after_ref, out_ref):
    small = mine_ref.shape[0]
    for step, block in ((0, mine_ref), (2, far_ref), (3, before_ref), (1, after_ref)):
        at = pl.multiple_of(lax.rem(slot_ref[0] + step, SIDE) * small, small)
        out_ref[pl.ds(at, small), :] = block[...]


def in_order(blocks, place):
    small, units = blocks[0].shape
    tile = units // 3
    grid = pltpu.PrefetchScalarGridSpec(
        num_scalar_prefetch=1,
        grid=(3,),
        in_specs=[pl.BlockSpec((small, tile), lambda j, slot: (0, j))] * 4,
        out_specs=pl.BlockSpec((SIDE * small, tile), lambda j, slot: (0, j)),
    )
    return pl.pallas_call(
        put_kernel,
        grid_spec=grid,
        out_shape=jax.ShapeDtypeStruct((SIDE * small, units), BF16),
        cost_estimate=COST,
        name="in_order",
    )(place.reshape(1), *blocks)


def in_hbm(a):
    return pltpu.with_memory_space_constraint(a, pltpu.HBM)


class Shares:
    def __init__(self, tensor, held, weight):
        self.tensor, self.weight = tensor, weight
        self.small, self.width = held[0].shape[3:]
        self.units = weight.shape[1 - tensor]
        self.tile = self.units // TILES
        self.big = SIDE * self.small

    def rows_spec(self, step):
        def along_x(j, slot):
            return (lax.rem(slot[0] + step, SIDE), 0, 0, 0, 0)

        def along_y(j, slot):
            return (0, 1, lax.rem(lax.rem(slot[0] + step, SIDE), 2), 0, 0)

        if self.tensor == 0:
            return pl.BlockSpec((1, 1, 2, self.small, self.width), along_x)
        return pl.BlockSpec((SIDE, 1, 1, self.small, self.width), along_y)

    def weight_spec(self):
        if self.tensor == 0:
            return pl.BlockSpec((self.width, self.tile), lambda j, slot: (0, j))
        return pl.BlockSpec((self.tile, self.width), lambda j, slot: (j, 0))

    def call(self, kernel, place, held, steps, outs, specs, name):
        grid = pltpu.PrefetchScalarGridSpec(
            num_scalar_prefetch=1,
            grid=(TILES,),
            in_specs=[self.rows_spec(step) for step in steps for _ in held] + [self.weight_spec()],
            out_specs=specs,
        )
        return pl.pallas_call(
            functools.partial(kernel, self.tensor),
            grid_spec=grid,
            out_shape=outs,
            compiler_params=pltpu.CompilerParams(vmem_limit_bytes=24 * 1024 * 1024),
            cost_estimate=COST,
            name=name,
        )(place.reshape(1), *(held * len(steps)), in_hbm(self.weight))

    def far(self, place, held):
        half = jax.ShapeDtypeStruct((self.big, self.units // 2), BF16)
        last = TILES // 2 - 1
        shape = (self.big, self.tile)
        specs = [
            pl.BlockSpec(shape, lambda j, slot: (0, jnp.minimum(j, last))),
            pl.BlockSpec(shape, lambda j, slot: (0, jnp.maximum(j - last - 1, 0))),
        ]
        return self.call(far_kernel, place, held, (2,), [half, half], specs, "far_share")

    def near(self, place, held):
        whole = (self.big, self.units)
        outs = [pltpu.HBM(whole, BF16)] * 3
        specs = [pl.BlockSpec((self.big, self.tile), lambda j, slot: (0, j))] * 3
        return self.call(near_kernel, place, held, (1, 3, 0), outs, specs, "near_shares")

    def add(self, place, after, before, got):
        block = (self.big, self.tile)
        first = pl.BlockSpec(block, lambda j, slot: (0, j))
        second = pl.BlockSpec(block, lambda j, slot: (0, j + TILES // 2))
        grid = pltpu.PrefetchScalarGridSpec(
            num_scalar_prefetch=1,
            grid=(TILES // 2,),
            in_specs=[first, second, first, first],
            out_specs=[first, second],
        )
        return pl.pallas_call(
            add_kernel,
            grid_spec=grid,
            out_shape=[pltpu.HBM(after.shape, BF16)] * 2,
            input_output_aliases={1: 0, 2: 1},
            cost_estimate=COST,
            name="add_far",
        )(place.reshape(1), in_hbm(after), in_hbm(before), *got)


def steps_on(axis, step):
    if axis == "x":
        return [(4 * x + y, 4 * ((x + step) % 4) + y) for x in range(4) for y in range(4)]
    if axis == "y":
        return [(4 * x + y, 4 * x + (y + step) % 4) for x in range(4) for y in range(4)]
    if axis == "z":
        return [(2 * z + c, 2 * ((z + step) % 4) + c) for z in range(4) for c in range(2)]
    return [(r, r ^ 1) for r in range(8)]


def send(a, axis, step):
    return lax.ppermute(a, "col" if axis in ("x", "y") else "row", steps_on(axis, step))


def trade(*sends):
    held = lax.optimization_barrier([a for a, _, _ in sends])
    return [send(a, axis, step) for a, (_, axis, step) in zip(held, sends)]


def gate(value, *earlier):
    return lax.optimization_barrier((value, earlier))[0]


def wide_gather(mine, place, axis):
    n = mine.shape[0] // 2
    before, after = trade((mine, axis, 1), (mine, axis, -1))
    far = trade((before[:n], axis, 1), (after[n:], axis, -1))
    return [
        (place, 0, mine),
        (place + 3, 0, before),
        (place + 1, 0, after),
        (place + 2, 0, far[0]),
        (place + 2, n, far[1]),
    ]


def local(x_values, x_scales, up_weight, down_weight, grad_values, grad_scales):
    col = lax.axis_index("col")
    x, y = col // SIDE, lax.rem(col, SIDE)
    n, width = x_values.shape
    small, tokens, units = n // 2, 8 * n, up_weight.shape[1]
    big, cut = tokens // SIDE, units // 2

    own = scaled(x_values, x_scales, grad_values, grad_scales)
    far, above, below = trade((own, "z", 2), (own, "z", -1), (own, "z", 1))
    same = jnp.concatenate([own, above, far, below], axis=0)
    held = [a.reshape(SIDE, 2, 2, small, width) for a in (same, send(same, "core", 1))]
    up, down = Shares(0, held, up_weight), Shares(1, held, down_weight)
    x_far = up.far(x, held)
    x_got = trade((x_far[0], "x", 1), (x_far[1], "x", -1))
    g_far = down.far(gate(y, x_far[0]), held)
    g_got = trade((g_far[0], "y", 1), (g_far[1], "y", -1))
    *x_near, x_mine = up.near(gate(x, g_far[0]), held)
    *g_near, g_mine = down.near(gate(y, x_mine), held)
    x_near = up.add(gate(x, g_mine), *x_near, x_got)
    x_got = trade((x_near[0], "x", 1), (x_near[1], "x", -1))
    g_near = down.add(gate(y, x_near[0]), *g_near, g_got)
    g_got = trade((g_near[0], "y", 1), (g_near[1], "y", -1))
    crossed = jnp.stack(held)[:, :, 0].transpose(0, 2, 1, 3, 4).reshape(tokens, width)

    def narrow(terms, place, axis):
        far, after, before, mine = row_blocks(terms, place)
        return [mine] + trade((far, axis, 2), (after, axis, 1), (before, axis, -1))

    def gather_narrow(mine, place, axis):
        got = trade((mine, axis, 2), (mine, axis, 1), (mine, axis, -1))
        return in_order([mine] + got, place)

    pre, hidden = by_tiles(act_kernel, narrow([x_mine] + x_got, y, "y"), (F32, BF16), "act")
    grad = narrow([g_mine] + g_got, x, "x")
    (grad_pre,) = by_tiles(slope_kernel, grad + [pre], (BF16,), "slope")
    hidden = wide_gather(gather_narrow(hidden, y, "y"), x, "x")
    grad_pre = wide_gather(gather_narrow(grad_pre, x, "x"), y, "y")

    terms = jnp.zeros((tokens, width), F32)
    for slot, ahead, block in hidden:
        term = jnp.dot(block, down_weight, preferred_element_type=F32)
        terms = lax.dynamic_update_slice_in_dim(terms, term, lax.rem(slot, SIDE) * big + ahead, 0)
    terms = terms.reshape(SIDE, 2, n, width)
    other = send(terms[:, 1].astype(BF16).reshape(tokens // 2, width), "core", 1)
    mine = terms[:, 0] + other.astype(F32).reshape(SIDE, n, width)
    sends = mine.astype(BF16)
    got = trade((sends[2], "z", 2), (sends[1], "z", 1), (sends[3], "z", -1))
    output = mine[0] + got[0].astype(F32) + got[1].astype(F32) + got[2].astype(F32)

    whole = jnp.zeros((tokens, units), BF16)
    for slot, ahead, block in grad_pre:
        whole = lax.dynamic_update_slice_in_dim(whole, block, lax.rem(slot, SIDE) * big + ahead, 0)
    up_grad = lax.dot_general(
        crossed, whole, (((0,), (0,)), ((), ())), preferred_element_type=F32
    )
    return (output.astype(BF16), up_grad)


def solution(mesh):
    placed = (
        P("row", "col"),
        P("col", "row"),
        P("col", "row"),
        P("row", "col"),
        P("row", "col"),
        P("col", "row"),
    )
    return jax.shard_map(
        local,
        mesh=mesh,
        in_specs=placed,
        out_specs=(P("row", "col"), P("col", "row")),
        check_vma=False,
    )
```

```python
import functools

import jax
import jax.numpy as jnp
from jax import lax
from jax.experimental import pallas as pl
from jax.experimental.pallas import tpu as pltpu
from jax.sharding import PartitionSpec as P

BLOCK = 128
SIDE = 4
TILES = 6
PIECES = 3
BF16 = jnp.bfloat16
F32 = jnp.float32
COST = pl.CostEstimate(flops=1000, bytes_accessed=1000, transcendentals=0)


def gelu(v):
    return 0.5 * v * (1.0 + jnp.tanh(0.7978845608 * (v + 0.044715 * v * v * v)))


def gelu_slope(v):
    return jax.vjp(gelu, v)[1](jnp.ones_like(v))[0]


def scale_kernel(xv_ref, xs_ref, gv_ref, gs_ref, out_ref):
    n = xv_ref.shape[0]
    i = lax.broadcasted_iota(jnp.int32, (n, n), 0)
    diagonal = i == lax.broadcasted_iota(jnp.int32, (n, n), 1)
    for t, (values, scales) in enumerate(((xv_ref, xs_ref), (gv_ref, gs_ref))):
        for b in range(values.shape[1] // BLOCK):
            at = slice(b * BLOCK, (b + 1) * BLOCK)
            row = scales[b : b + 1, :].astype(F32)
            weight = jnp.where(diagonal, jnp.broadcast_to(row, (n, n)), 0.0).astype(BF16)
            block = jnp.dot(weight, values[:, at], preferred_element_type=F32)
            out_ref[t * n : (t + 1) * n, at] = block.astype(BF16)


def scaled(x_values, x_scales, grad_values, grad_scales):
    n, width = x_values.shape
    return pl.pallas_call(
        scale_kernel, out_shape=jax.ShapeDtypeStruct((2 * n, width), BF16), name="scale"
    )(x_values, x_scales, grad_values, grad_scales)


def share_dot(tensor, take, same_ref, other_ref, w_refs):
    width = same_ref.shape[-1]
    if tensor == 0:
        a = jnp.concatenate([r[...].reshape(-1, width) for r in (same_ref, other_ref)], axis=0)
    else:
        a = jnp.where(take == 0, same_ref[...], other_ref[...]).reshape(-1, width)
    dims = (((1,), (tensor,)), ((), ()))
    n = width // len(w_refs)
    return sum(
        lax.dot_general(a[:, k * n : (k + 1) * n], w[...], dims, preferred_element_type=F32)
        for k, w in enumerate(w_refs)
    )


def core_of(slot_ref, step):
    return lax.div(lax.rem(slot_ref[0] + step, SIDE), 2)


def far_kernel(tensor, slot_ref, same_ref, other_ref, *refs):
    w_refs, (low_ref, high_ref) = refs[:PIECES], refs[PIECES:]
    j, half = pl.program_id(0), pl.num_programs(0) // 2
    out = share_dot(tensor, core_of(slot_ref, 2), same_ref, other_ref, w_refs).astype(BF16)

    @pl.when(j < half)
    def _():
        low_ref[...] = out

    @pl.when(j >= half)
    def _():
        high_ref[...] = out


def near_kernel(tensor, slot_ref, *refs):
    w_refs, outs = refs[6 : 6 + PIECES], refs[6 + PIECES :]
    for i, step in enumerate((1, 3, 0)):
        same_ref, other_ref = refs[2 * i : 2 * i + 2]
        out = share_dot(tensor, core_of(slot_ref, step), same_ref, other_ref, w_refs)
        outs[i][...] = out.astype(BF16)


def add_kernel(slot_ref, after_ref, before_ref, low_ref, high_ref, after_out, before_out):
    after_out[...] = (after_ref[...].astype(F32) + low_ref[...].astype(F32)).astype(BF16)
    before_out[...] = (before_ref[...].astype(F32) + high_ref[...].astype(F32)).astype(BF16)


def blocks_kernel(slot_ref, *refs):
    ins, outs = refs[: 3 * SIDE], refs[3 * SIDE :]
    for i, out in enumerate(outs):
        out[...] = sum(r[...].astype(F32) for r in ins[3 * i : 3 * i + 3]).astype(out.dtype)


def row_blocks(terms, place):
    big, units = terms[0].shape
    shape = (big // SIDE, units // 2)
    ins = [
        pl.BlockSpec(shape, lambda j, slot, step=step: (lax.rem(slot[0] + step, SIDE), j))
        for step in (2, 1, 3, 0)
    ]
    grid = pltpu.PrefetchScalarGridSpec(
        num_scalar_prefetch=1,
        grid=(2,),
        in_specs=[spec for spec in ins for _ in range(3)],
        out_specs=[pl.BlockSpec(shape, lambda j, slot: (0, j))] * 4,
    )
    return pl.pallas_call(
        blocks_kernel,
        grid_spec=grid,
        out_shape=[pltpu.HBM((big // SIDE, units), kind) for kind in (BF16, BF16, BF16, F32)],
        cost_estimate=COST,
        name="row_blocks",
    )(place.reshape(1), *(list(terms) * SIDE))


def act_kernel(a_ref, b_ref, c_ref, d_ref, pre_ref, hidden_ref):
    pre = a_ref[...] + sum(r[...].astype(F32) for r in (b_ref, c_ref, d_ref))
    pre_ref[...] = pre
    hidden_ref[...] = gelu(pre).astype(BF16)


def slope_kernel(a_ref, b_ref, c_ref, d_ref, pre_ref, out_ref):
    grad = a_ref[...] + sum(r[...].astype(F32) for r in (b_ref, c_ref, d_ref))
    out_ref[...] = (grad * gelu_slope(pre_ref[...])).astype(BF16)


def by_tiles(kernel, ins, kinds, name):
    rows_in, units = ins[0].shape
    spec = pl.BlockSpec((rows_in, units // 3), lambda j: (0, j))
    return pl.pallas_call(
        kernel,
        grid=(3,),
        in_specs=[spec] * len(ins),
        out_specs=[spec] * len(kinds),
        out_shape=[jax.ShapeDtypeStruct((rows_in, units), kind) for kind in kinds],
        cost_estimate=COST,
        name=name,
    )(*ins)


def put_kernel(slot_ref, mine_ref, far_ref, before_ref, after_ref, out_ref):
    small = mine_ref.shape[0]
    for step, block in ((0, mine_ref), (2, far_ref), (3, before_ref), (1, after_ref)):
        at = pl.multiple_of(lax.rem(slot_ref[0] + step, SIDE) * small, small)
        out_ref[pl.ds(at, small), :] = block[...]


def in_order(blocks, place):
    small, units = blocks[0].shape
    tile = units // 3
    grid = pltpu.PrefetchScalarGridSpec(
        num_scalar_prefetch=1,
        grid=(3,),
        in_specs=[pl.BlockSpec((small, tile), lambda j, slot: (0, j))] * 4,
        out_specs=pl.BlockSpec((SIDE * small, tile), lambda j, slot: (0, j)),
    )
    return pl.pallas_call(
        put_kernel,
        grid_spec=grid,
        out_shape=jax.ShapeDtypeStruct((SIDE * small, units), BF16),
        cost_estimate=COST,
        name="in_order",
    )(place.reshape(1), *blocks)


def in_hbm(a):
    return pltpu.with_memory_space_constraint(a, pltpu.HBM)


class Shares:
    def __init__(self, tensor, held, weight):
        self.tensor, self.weight = tensor, weight
        self.small, self.width = held[0].shape[3:]
        self.units = weight.shape[1 - tensor]
        self.tile = self.units // TILES
        self.big = SIDE * self.small

    def rows_spec(self, step):
        def along_x(j, slot):
            return (lax.rem(slot[0] + step, SIDE), 0, 0, 0, 0)

        def along_y(j, slot):
            return (0, 1, lax.rem(lax.rem(slot[0] + step, SIDE), 2), 0, 0)

        if self.tensor == 0:
            return pl.BlockSpec((1, 1, 2, self.small, self.width), along_x)
        return pl.BlockSpec((SIDE, 1, 1, self.small, self.width), along_y)

    def weight_specs(self):
        n = self.width // PIECES
        if self.tensor == 0:
            return [
                pl.BlockSpec((n, self.tile), lambda j, slot, k=k: (k, j)) for k in range(PIECES)
            ]
        return [pl.BlockSpec((self.tile, n), lambda j, slot, k=k: (j, k)) for k in range(PIECES)]

    def call(self, kernel, place, held, steps, outs, specs, name):
        grid = pltpu.PrefetchScalarGridSpec(
            num_scalar_prefetch=1,
            grid=(TILES,),
            in_specs=[self.rows_spec(step) for step in steps for _ in held] + self.weight_specs(),
            out_specs=specs,
        )
        return pl.pallas_call(
            functools.partial(kernel, self.tensor),
            grid_spec=grid,
            out_shape=outs,
            compiler_params=pltpu.CompilerParams(vmem_limit_bytes=24 * 1024 * 1024),
            cost_estimate=COST,
            name=name,
        )(place.reshape(1), *(held * len(steps)), *([in_hbm(self.weight)] * PIECES))

    def far(self, place, held):
        half = pltpu.HBM((self.big, self.units // 2), BF16)
        last = TILES // 2 - 1
        shape = (self.big, self.tile)
        specs = [
            pl.BlockSpec(shape, lambda j, slot: (0, jnp.minimum(j, last))),
            pl.BlockSpec(shape, lambda j, slot: (0, jnp.maximum(j - last - 1, 0))),
        ]
        return self.call(far_kernel, place, held, (2,), [half, half], specs, "far_share")

    def near(self, place, held):
        whole = (self.big, self.units)
        outs = [pltpu.HBM(whole, BF16)] * 3
        specs = [pl.BlockSpec((self.big, self.tile), lambda j, slot: (0, j))] * 3
        return self.call(near_kernel, place, held, (1, 3, 0), outs, specs, "near_shares")

    def add(self, place, after, before, got):
        block = (self.big, self.tile)
        first = pl.BlockSpec(block, lambda j, slot: (0, j))
        second = pl.BlockSpec(block, lambda j, slot: (0, j + TILES // 2))
        grid = pltpu.PrefetchScalarGridSpec(
            num_scalar_prefetch=1,
            grid=(TILES // 2,),
            in_specs=[first, second, first, first],
            out_specs=[first, second],
        )
        return pl.pallas_call(
            add_kernel,
            grid_spec=grid,
            out_shape=[pltpu.HBM(after.shape, BF16)] * 2,
            input_output_aliases={1: 0, 2: 1},
            cost_estimate=COST,
            name="add_far",
        )(place.reshape(1), in_hbm(after), in_hbm(before), *got)


def steps_on(axis, step):
    if axis == "x":
        return [(4 * x + y, 4 * ((x + step) % 4) + y) for x in range(4) for y in range(4)]
    if axis == "y":
        return [(4 * x + y, 4 * x + (y + step) % 4) for x in range(4) for y in range(4)]
    if axis == "z":
        return [(2 * z + c, 2 * ((z + step) % 4) + c) for z in range(4) for c in range(2)]
    return [(r, r ^ 1) for r in range(8)]


def send(a, axis, step):
    return lax.ppermute(a, "col" if axis in ("x", "y") else "row", steps_on(axis, step))


def trade(*sends):
    held = lax.optimization_barrier([a for a, _, _ in sends])
    return [send(a, axis, step) for a, (_, axis, step) in zip(held, sends)]


def gate(value, *earlier):
    return lax.optimization_barrier((value, earlier))[0]


def wide_gather(mine, place, axis):
    n = mine.shape[0] // 2
    before, after = trade((mine, axis, 1), (mine, axis, -1))
    far = trade((before[:n], axis, 1), (after[n:], axis, -1))
    return [
        (place, 0, mine),
        (place + 3, 0, before),
        (place + 1, 0, after),
        (place + 2, 0, far[0]),
        (place + 2, n, far[1]),
    ]


def local(x_values, x_scales, up_weight, down_weight, grad_values, grad_scales):
    col = lax.axis_index("col")
    x, y = col // SIDE, lax.rem(col, SIDE)
    n, width = x_values.shape
    small, tokens, units = n // 2, 8 * n, up_weight.shape[1]
    big, cut = tokens // SIDE, units // 2

    own = scaled(x_values, x_scales, grad_values, grad_scales)
    far, above, below = trade((own, "z", 2), (own, "z", -1), (own, "z", 1))
    same = jnp.concatenate([own, above, far, below], axis=0)
    held = [a.reshape(SIDE, 2, 2, small, width) for a in (same, send(same, "core", 1))]
    up, down = Shares(0, held, up_weight), Shares(1, held, down_weight)
    x_far = up.far(x, held)
    x_got = trade((x_far[0], "x", 1), (x_far[1], "x", -1))
    g_far = down.far(gate(y, x_far[0]), held)
    g_got = trade((g_far[0], "y", 1), (g_far[1], "y", -1))
    *x_near, x_mine = up.near(gate(x, g_far[0]), held)
    *g_near, g_mine = down.near(gate(y, x_mine), held)
    x_near = up.add(gate(x, g_mine), *x_near, x_got)
    x_got = trade((x_near[0], "x", 1), (x_near[1], "x", -1))
    g_near = down.add(gate(y, x_near[0]), *g_near, g_got)
    g_got = trade((g_near[0], "y", 1), (g_near[1], "y", -1))
    crossed = jnp.stack(held)[:, :, 0].transpose(0, 2, 1, 3, 4).reshape(tokens, width)

    def narrow(terms, place, axis):
        far, after, before, mine = row_blocks(terms, place)
        return [mine] + trade((far, axis, 2), (after, axis, 1), (before, axis, -1))

    def gather_narrow(mine, place, axis):
        got = trade((mine, axis, 2), (mine, axis, 1), (mine, axis, -1))
        return in_order([mine] + got, place)

    pre, hidden = by_tiles(act_kernel, narrow([x_mine] + x_got, y, "y"), (F32, BF16), "act")
    grad = narrow([g_mine] + g_got, x, "x")
    (grad_pre,) = by_tiles(slope_kernel, grad + [pre], (BF16,), "slope")
    hidden = wide_gather(gather_narrow(hidden, y, "y"), x, "x")
    grad_pre = wide_gather(gather_narrow(grad_pre, x, "x"), y, "y")

    terms = jnp.zeros((tokens, width), F32)
    for slot, ahead, block in hidden:
        term = jnp.dot(block, down_weight, preferred_element_type=F32)
        terms = lax.dynamic_update_slice_in_dim(terms, term, lax.rem(slot, SIDE) * big + ahead, 0)
    terms = terms.reshape(SIDE, 2, n, width)
    other = send(terms[:, 1].astype(BF16).reshape(tokens // 2, width), "core", 1)
    mine = terms[:, 0] + other.astype(F32).reshape(SIDE, n, width)
    sends = mine.astype(BF16)
    got = trade((sends[2], "z", 2), (sends[1], "z", 1), (sends[3], "z", -1))
    output = mine[0] + got[0].astype(F32) + got[1].astype(F32) + got[2].astype(F32)

    whole = jnp.zeros((tokens, units), BF16)
    for slot, ahead, block in grad_pre:
        whole = lax.dynamic_update_slice_in_dim(whole, block, lax.rem(slot, SIDE) * big + ahead, 0)
    up_grad = lax.dot_general(
        crossed, whole, (((0,), (0,)), ((), ())), preferred_element_type=F32
    )
    return (output.astype(BF16), up_grad)


def solution(mesh):
    placed = (
        P("row", "col"),
        P("col", "row"),
        P("col", "row"),
        P("row", "col"),
        P("row", "col"),
        P("col", "row"),
    )
    return jax.shard_map(
        local,
        mesh=mesh,
        in_specs=placed,
        out_specs=(P("row", "col"), P("col", "row")),
        check_vma=False,
    )
```

```python
import functools

import jax
import jax.numpy as jnp
from jax import lax
from jax.experimental import pallas as pl
from jax.experimental.pallas import tpu as pltpu
from jax.sharding import PartitionSpec as P

BLOCK = 128
SIDE = 4
TILES = 6
PIECES = 3
BF16 = jnp.bfloat16
F32 = jnp.float32
SMALL = pltpu.CompilerParams(vmem_limit_bytes=10 * 1024 * 1024)
COST = pl.CostEstimate(flops=1000, bytes_accessed=1000, transcendentals=0)


def gelu(v):
    return 0.5 * v * (1.0 + jnp.tanh(0.7978845608 * (v + 0.044715 * v * v * v)))


def gelu_slope(v):
    return jax.vjp(gelu, v)[1](jnp.ones_like(v))[0]


def scale_kernel(xv_ref, xs_ref, gv_ref, gs_ref, out_ref):
    n = xv_ref.shape[0]
    i = lax.broadcasted_iota(jnp.int32, (n, n), 0)
    diagonal = i == lax.broadcasted_iota(jnp.int32, (n, n), 1)
    for t, (values, scales) in enumerate(((xv_ref, xs_ref), (gv_ref, gs_ref))):
        for b in range(values.shape[1] // BLOCK):
            at = slice(b * BLOCK, (b + 1) * BLOCK)
            row = scales[b : b + 1, :].astype(F32)
            weight = jnp.where(diagonal, jnp.broadcast_to(row, (n, n)), 0.0).astype(BF16)
            block = jnp.dot(weight, values[:, at], preferred_element_type=F32)
            out_ref[t * n : (t + 1) * n, at] = block.astype(BF16)


def scaled(x_values, x_scales, grad_values, grad_scales):
    n, width = x_values.shape
    return pl.pallas_call(
        scale_kernel, out_shape=jax.ShapeDtypeStruct((2 * n, width), BF16), name="scale"
    )(x_values, x_scales, grad_values, grad_scales)


def share_dot(tensor, take, same_ref, other_ref, w_refs):
    width = same_ref.shape[-1]
    if tensor == 0:
        a = jnp.concatenate([r[...].reshape(-1, width) for r in (same_ref, other_ref)], axis=0)
    else:
        a = jnp.where(take == 0, same_ref[...], other_ref[...]).reshape(-1, width)
    dims = (((1,), (tensor,)), ((), ()))
    n = width // len(w_refs)
    return sum(
        lax.dot_general(a[:, k * n : (k + 1) * n], w[...], dims, preferred_element_type=F32)
        for k, w in enumerate(w_refs)
    )


def core_of(slot_ref, step):
    return lax.div(lax.rem(slot_ref[0] + step, SIDE), 2)


def far_kernel(tensor, slot_ref, same_ref, other_ref, *refs):
    w_refs, (low_ref, high_ref) = refs[:PIECES], refs[PIECES:]
    j, half = pl.program_id(0), pl.num_programs(0) // 2
    out = share_dot(tensor, core_of(slot_ref, 2), same_ref, other_ref, w_refs).astype(BF16)

    @pl.when(j < half)
    def _():
        low_ref[...] = out

    @pl.when(j >= half)
    def _():
        high_ref[...] = out


def near_kernel(tensor, slot_ref, *refs):
    w_refs, outs = refs[6 : 6 + PIECES], refs[6 + PIECES :]
    for i, step in enumerate((1, 3, 0)):
        same_ref, other_ref = refs[2 * i : 2 * i + 2]
        out = share_dot(tensor, core_of(slot_ref, step), same_ref, other_ref, w_refs)
        outs[i][...] = out.astype(BF16)


def add_kernel(slot_ref, after_ref, before_ref, low_ref, high_ref, after_out, before_out):
    after_out[...] = (after_ref[...].astype(F32) + low_ref[...].astype(F32)).astype(BF16)
    before_out[...] = (before_ref[...].astype(F32) + high_ref[...].astype(F32)).astype(BF16)


def blocks_kernel(slot_ref, *refs):
    ins, outs = refs[: 3 * SIDE], refs[3 * SIDE :]
    for i, out in enumerate(outs):
        out[...] = sum(r[...].astype(F32) for r in ins[3 * i : 3 * i + 3]).astype(out.dtype)


def row_blocks(terms, place):
    big, units = terms[0].shape
    shape = (big // SIDE, units // 2)
    ins = [
        pl.BlockSpec(shape, lambda j, slot, step=step: (lax.rem(slot[0] + step, SIDE), j))
        for step in (2, 1, 3, 0)
    ]
    grid = pltpu.PrefetchScalarGridSpec(
        num_scalar_prefetch=1,
        grid=(2,),
        in_specs=[spec for spec in ins for _ in range(3)],
        out_specs=[pl.BlockSpec(shape, lambda j, slot: (0, j))] * 4,
    )
    return pl.pallas_call(
        blocks_kernel,
        grid_spec=grid,
        out_shape=[pltpu.HBM((big // SIDE, units), kind) for kind in (BF16, BF16, BF16, F32)],
        compiler_params=SMALL,
        cost_estimate=COST,
        name="row_blocks",
    )(place.reshape(1), *(list(terms) * SIDE))


def act_kernel(a_ref, b_ref, c_ref, d_ref, pre_ref, hidden_ref):
    pre = a_ref[...] + sum(r[...].astype(F32) for r in (b_ref, c_ref, d_ref))
    pre_ref[...] = pre
    hidden_ref[...] = gelu(pre).astype(BF16)


def slope_kernel(a_ref, b_ref, c_ref, d_ref, pre_ref, out_ref):
    grad = a_ref[...] + sum(r[...].astype(F32) for r in (b_ref, c_ref, d_ref))
    out_ref[...] = (grad * gelu_slope(pre_ref[...])).astype(BF16)


def by_tiles(kernel, ins, kinds, name):
    rows_in, units = ins[0].shape
    spec = pl.BlockSpec((rows_in, units // 3), lambda j: (0, j))
    return pl.pallas_call(
        kernel,
        grid=(3,),
        in_specs=[spec] * len(ins),
        out_specs=[spec] * len(kinds),
        out_shape=[jax.ShapeDtypeStruct((rows_in, units), kind) for kind in kinds],
        compiler_params=SMALL,
        cost_estimate=COST,
        name=name,
    )(*ins)


def put_kernel(slot_ref, mine_ref, far_ref, before_ref, after_ref, out_ref):
    small = mine_ref.shape[0]
    for step, block in ((0, mine_ref), (2, far_ref), (3, before_ref), (1, after_ref)):
        at = pl.multiple_of(lax.rem(slot_ref[0] + step, SIDE) * small, small)
        out_ref[pl.ds(at, small), :] = block[...]


def in_order(blocks, place):
    small, units = blocks[0].shape
    tile = units // 3
    grid = pltpu.PrefetchScalarGridSpec(
        num_scalar_prefetch=1,
        grid=(3,),
        in_specs=[pl.BlockSpec((small, tile), lambda j, slot: (0, j))] * 4,
        out_specs=pl.BlockSpec((SIDE * small, tile), lambda j, slot: (0, j)),
    )
    return pl.pallas_call(
        put_kernel,
        grid_spec=grid,
        out_shape=jax.ShapeDtypeStruct((SIDE * small, units), BF16),
        compiler_params=SMALL,
        cost_estimate=COST,
        name="in_order",
    )(place.reshape(1), *blocks)


def in_hbm(a):
    return pltpu.with_memory_space_constraint(a, pltpu.HBM)


class Shares:
    def __init__(self, tensor, held, weight):
        self.tensor, self.weight = tensor, weight
        self.small, self.width = held[0].shape[3:]
        self.units = weight.shape[1 - tensor]
        self.tile = self.units // TILES
        self.big = SIDE * self.small

    def rows_spec(self, step):
        def along_x(j, slot):
            return (lax.rem(slot[0] + step, SIDE), 0, 0, 0, 0)

        def along_y(j, slot):
            return (0, 1, lax.rem(lax.rem(slot[0] + step, SIDE), 2), 0, 0)

        if self.tensor == 0:
            return pl.BlockSpec((1, 1, 2, self.small, self.width), along_x)
        return pl.BlockSpec((SIDE, 1, 1, self.small, self.width), along_y)

    def weight_specs(self):
        n = self.width // PIECES
        if self.tensor == 0:
            return [
                pl.BlockSpec((n, self.tile), lambda j, slot, k=k: (k, j)) for k in range(PIECES)
            ]
        return [pl.BlockSpec((self.tile, n), lambda j, slot, k=k: (j, k)) for k in range(PIECES)]

    def call(self, kernel, place, held, steps, outs, specs, name):
        grid = pltpu.PrefetchScalarGridSpec(
            num_scalar_prefetch=1,
            grid=(TILES,),
            in_specs=[self.rows_spec(step) for step in steps for _ in held] + self.weight_specs(),
            out_specs=specs,
        )
        return pl.pallas_call(
            functools.partial(kernel, self.tensor),
            grid_spec=grid,
            out_shape=outs,
            compiler_params=pltpu.CompilerParams(vmem_limit_bytes=16 * 1024 * 1024),
            cost_estimate=COST,
            name=name,
        )(place.reshape(1), *(held * len(steps)), *([in_hbm(self.weight)] * PIECES))

    def far(self, place, held):
        half = pltpu.HBM((self.big, self.units // 2), BF16)
        last = TILES // 2 - 1
        shape = (self.big, self.tile)
        specs = [
            pl.BlockSpec(shape, lambda j, slot: (0, jnp.minimum(j, last))),
            pl.BlockSpec(shape, lambda j, slot: (0, jnp.maximum(j - last - 1, 0))),
        ]
        return self.call(far_kernel, place, held, (2,), [half, half], specs, "far_share")

    def near(self, place, held):
        whole = (self.big, self.units)
        outs = [pltpu.HBM(whole, BF16)] * 3
        specs = [pl.BlockSpec((self.big, self.tile), lambda j, slot: (0, j))] * 3
        return self.call(near_kernel, place, held, (1, 3, 0), outs, specs, "near_shares")

    def add(self, place, after, before, got):
        block = (self.big, self.tile)
        first = pl.BlockSpec(block, lambda j, slot: (0, j))
        second = pl.BlockSpec(block, lambda j, slot: (0, j + TILES // 2))
        grid = pltpu.PrefetchScalarGridSpec(
            num_scalar_prefetch=1,
            grid=(TILES // 2,),
            in_specs=[first, second, first, first],
            out_specs=[first, second],
        )
        return pl.pallas_call(
            add_kernel,
            grid_spec=grid,
            out_shape=[pltpu.HBM(after.shape, BF16)] * 2,
            input_output_aliases={1: 0, 2: 1},
            compiler_params=SMALL,
            cost_estimate=COST,
            name="add_far",
        )(place.reshape(1), in_hbm(after), in_hbm(before), *got)


def steps_on(axis, step):
    if axis == "x":
        return [(4 * x + y, 4 * ((x + step) % 4) + y) for x in range(4) for y in range(4)]
    if axis == "y":
        return [(4 * x + y, 4 * x + (y + step) % 4) for x in range(4) for y in range(4)]
    if axis == "z":
        return [(2 * z + c, 2 * ((z + step) % 4) + c) for z in range(4) for c in range(2)]
    return [(r, r ^ 1) for r in range(8)]


def send(a, axis, step):
    return lax.ppermute(a, "col" if axis in ("x", "y") else "row", steps_on(axis, step))


def trade(*sends):
    held = lax.optimization_barrier([a for a, _, _ in sends])
    return [send(a, axis, step) for a, (_, axis, step) in zip(held, sends)]


def gate(value, *earlier):
    return lax.optimization_barrier((value, earlier))[0]


def wide_gather(mine, place, axis):
    n = mine.shape[0] // 2
    before, after = trade((mine, axis, 1), (mine, axis, -1))
    far = trade((before[:n], axis, 1), (after[n:], axis, -1))
    return [
        (place, 0, mine),
        (place + 3, 0, before),
        (place + 1, 0, after),
        (place + 2, 0, far[0]),
        (place + 2, n, far[1]),
    ]


def local(x_values, x_scales, up_weight, down_weight, grad_values, grad_scales):
    col = lax.axis_index("col")
    x, y = col // SIDE, lax.rem(col, SIDE)
    n, width = x_values.shape
    small, tokens, units = n // 2, 8 * n, up_weight.shape[1]
    big, cut = tokens // SIDE, units // 2

    own = scaled(x_values, x_scales, grad_values, grad_scales)
    far, above, below = trade((own, "z", 2), (own, "z", -1), (own, "z", 1))
    same = jnp.concatenate([own, above, far, below], axis=0)
    held = [a.reshape(SIDE, 2, 2, small, width) for a in (same, send(same, "core", 1))]
    up, down = Shares(0, held, up_weight), Shares(1, held, down_weight)
    x_far = up.far(x, held)
    x_got = trade((x_far[0], "x", 1), (x_far[1], "x", -1))
    g_far = down.far(gate(y, x_far[0]), held)
    g_got = trade((g_far[0], "y", 1), (g_far[1], "y", -1))
    *x_near, x_mine = up.near(gate(x, g_far[0]), held)
    *g_near, g_mine = down.near(gate(y, x_mine), held)
    x_near = up.add(gate(x, g_mine), *x_near, x_got)
    x_got = trade((x_near[0], "x", 1), (x_near[1], "x", -1))
    g_near = down.add(gate(y, x_near[0]), *g_near, g_got)
    g_got = trade((g_near[0], "y", 1), (g_near[1], "y", -1))
    crossed = jnp.stack(held)[:, :, 0].transpose(0, 2, 1, 3, 4).reshape(tokens, width)

    def narrow(terms, place, axis):
        far, after, before, mine = row_blocks(terms, place)
        return [mine] + trade((far, axis, 2), (after, axis, 1), (before, axis, -1))

    def gather_narrow(mine, place, axis):
        got = trade((mine, axis, 2), (mine, axis, 1), (mine, axis, -1))
        return in_order([mine] + got, place)

    pre, hidden = by_tiles(act_kernel, narrow([x_mine] + x_got, y, "y"), (F32, BF16), "act")
    grad = narrow([g_mine] + g_got, x, "x")
    (grad_pre,) = by_tiles(slope_kernel, grad + [pre], (BF16,), "slope")
    hidden = wide_gather(gather_narrow(hidden, y, "y"), x, "x")
    grad_pre = wide_gather(gather_narrow(grad_pre, x, "x"), y, "y")

    terms = jnp.zeros((tokens, width), F32)
    for slot, ahead, block in hidden:
        term = jnp.dot(block, down_weight, preferred_element_type=F32)
        terms = lax.dynamic_update_slice_in_dim(terms, term, lax.rem(slot, SIDE) * big + ahead, 0)
    terms = terms.reshape(SIDE, 2, n, width)
    other = send(terms[:, 1].astype(BF16).reshape(tokens // 2, width), "core", 1)
    mine = terms[:, 0] + other.astype(F32).reshape(SIDE, n, width)
    sends = mine.astype(BF16)
    got = trade((sends[2], "z", 2), (sends[1], "z", 1), (sends[3], "z", -1))
    output = mine[0] + got[0].astype(F32) + got[1].astype(F32) + got[2].astype(F32)

    whole = jnp.zeros((tokens, units), BF16)
    for slot, ahead, block in grad_pre:
        whole = lax.dynamic_update_slice_in_dim(whole, block, lax.rem(slot, SIDE) * big + ahead, 0)
    up_grad = lax.dot_general(
        crossed, whole, (((0,), (0,)), ((), ())), preferred_element_type=F32
    )
    return (output.astype(BF16), up_grad)


def solution(mesh):
    placed = (
        P("row", "col"),
        P("col", "row"),
        P("col", "row"),
        P("row", "col"),
        P("row", "col"),
        P("col", "row"),
    )
    return jax.shard_map(
        local,
        mesh=mesh,
        in_specs=placed,
        out_specs=(P("row", "col"), P("col", "row")),
        check_vma=False,
    )
```
